32 devices in a mesh: gz: 4 (over y, core), xy: 8 (over z, x).
Axes of the slice: x: 2, y: 2, z: 4, core: 2. Of those that a mesh axis runs over, the one named last changes fastest.
Arguments:
- cotangent: bfloat16 [4, 8, 9, 128, 128], P('gz', 'xy'), may hold values from -6 to 6
- displacement: float32 [4, 8, 3, 32, 128], P('gz', 'xy'), may hold values from -2 to 2
- neighbours: int32 [4, 8, 32, 128], P('gz', 'xy'), may hold values from 0 to 2303
- counts: int32 [4, 8, 128], P('gz', 'xy'), may hold values from 8 to 32, as said below
- atom_feat: bfloat16 [4, 8, 256, 128], P('gz', 'xy'), may hold values from -6 to 6
- radial_weight: float32 [3, 16, 128], replicated, may hold values from -1.5 to 1.5
- mix_weight: bfloat16 [3, 128, 128], replicated, may hold values from -0.5 to 0.5
Outputs:
- atom_grad: float32 [4, 8, 256, 128], P('gz', 'xy')
- radial_grad: float32 [3, 16, 128], replicated
- mix_grad: float32 [3, 128, 128], replicated
The draws below stay inside these ranges and needn't reach their ends.
Inputs may be any that keep to these rules, and one draw needn't show every extreme that they name: `counts`: the first probe of the first brick uses all 32 slots and the first probe of the second brick uses 32 // 4.
All inputs are finite; a program needn't handle non-finite values.
Results may differ from the reference program's by a relative error of at most 0.0051.
Values may be sent and summed in bfloat16 or wider, within the bound.
A program may use at most 64 MiB of HBM per device.

```python
import math
import jax
import jax.numpy as jnp
from jax import lax

CH = 128
NB = 16
K = 32
P_DEV = 128
A_DEV = 256
GROUPS = 4
BRICKS = 8


def draw_counts(key, part):
    first_key, second_key = jax.random.split(key)
    nbrick = GROUPS * BRICKS
    tops = jax.random.randint(first_key, (nbrick,), K // 2, K + 1)
    tops = tops.at[0].set(K).at[1].set(K // 2)
    bottoms = tops // 2
    values = jax.random.randint(second_key, (nbrick, P_DEV), bottoms[:, None], tops[:, None] + 1)
    values = values.at[0, 0].set(K).at[1, 0].set(K // 4)
    return values.reshape(GROUPS, BRICKS, P_DEV).astype(jnp.int32)


def plant(entries, key, low, high):
    longest = entries.shape.index(max(entries.shape))
    spots = []
    for shift in (0, 1):
        where = [jax.random.randint(jax.random.fold_in(key, axis), (), 0, length) for axis, length in enumerate(entries.shape)]
        where[longest] = (where[longest] + shift) % entries.shape[longest]
        spots.append(tuple(where))
    return entries.at[spots[0]].set(low).at[spots[1]].set(high)


def block_levels(own_key, extent, pieces, least, top_value):
    def one(dim, parts):
        steps = jax.random.uniform(jax.random.fold_in(jax.random.fold_in(own_key, 6), dim), (parts,), jnp.float32, least / len(pieces), top_value / len(pieces))
        return jnp.repeat(jnp.exp(steps), extent[dim] // parts).reshape((-1,) + (1,) * (len(extent) - dim - 1))

    loudness = one(*pieces[0])
    for cut in pieces[1:]:
        loudness = loudness * one(*cut)
    return loudness


def scatter_about(rng, extent, spread, bound, cuts=(), kind=jnp.bfloat16):
    entries = spread * jax.random.normal(rng, extent, jnp.float32)
    if cuts:
        entries = entries * block_levels(rng, extent, cuts, -0.22, 0.18)
    return jnp.clip(entries, -bound, bound).astype(kind)


def setup_inputs(seed: int = 0) -> dict:
    splits = jax.random.split(jax.random.key(seed), 8)
    cotangent = scatter_about(splits[0], (GROUPS, BRICKS, 9, P_DEV, CH), 1.0, 6.0, ((0, 4), (1, 8)))
    displacement = jnp.clip(jax.random.uniform(splits[1], (GROUPS, BRICKS, 3, K, P_DEV), jnp.float32, -2.0, 2.0) * block_levels(splits[1], (GROUPS, BRICKS, 3, K, P_DEV), ((0, 4), (1, 8)), -0.4, 0.0), -2.0, 2.0)
    neighbours = plant(jax.random.randint(splits[2], (GROUPS, BRICKS, K, P_DEV), 0, 9 * A_DEV), jax.random.fold_in(splits[2], 1), 0, (9 * A_DEV) - 1).astype(jnp.int32)
    counts = draw_counts(jax.random.fold_in(splits[7], 71), 0)
    atom_feat = scatter_about(splits[4], (GROUPS, BRICKS, A_DEV, CH), 1.0, 6.0, ((0, 4), (1, 8)))
    radial_weight = scatter_about(splits[5], (3, NB, CH), NB ** -0.5, 1.5, (), jnp.float32)
    mix_weight = scatter_about(splits[6], (3, CH, CH), CH ** -0.5, 0.5)
    return dict(cotangent=cotangent, displacement=displacement, neighbours=neighbours, counts=counts, atom_feat=atom_feat, radial_weight=radial_weight, mix_weight=mix_weight)


CUTOFF = 4.0
LEVEL_SPANS = ((0, 1), (1, 4), (4, 9))

def harmonics(disp):
    scaled = disp / CUTOFF
    coord_x, coord_y, coord_z = (scaled[0], scaled[1], scaled[2])
    root3, root5, root15 = (math.sqrt(3.0), math.sqrt(5.0), math.sqrt(15.0))
    return jnp.stack([jnp.ones_like(coord_x), root3 * coord_x, root3 * coord_y, root3 * coord_z, root15 * coord_x * coord_y, root15 * coord_y * coord_z, 0.5 * root5 * (2.0 * coord_z * coord_z - coord_x * coord_x - coord_y * coord_y), root15 * coord_x * coord_z, 0.5 * root15 * (coord_x * coord_x - coord_y * coord_y)])

def basis(disp, nbasis):
    distance = jnp.sqrt(lax.optimization_barrier(jnp.sum(disp * disp, axis=0)))
    centres = jnp.arange(nbasis).astype(jnp.float32) * (CUTOFF / (nbasis - 1))
    sharpness = ((nbasis - 1) / CUTOFF) ** 2
    envelope = 0.5 * (jnp.cos(math.pi * distance / CUTOFF) + 1.0)
    shaped = centres.reshape((nbasis,) + (1,) * distance.ndim)
    return jnp.exp(-sharpness * (distance[None] - shaped) ** 2) * envelope[None]

def product(form, left, right):
    return jnp.einsum(form, left.astype(jnp.float32), right.astype(jnp.float32), precision=lax.Precision.HIGHEST)

def gate_backward(moments, mix_weight, cotangent):
    mixed_out = [product('mpc,cd->mpd', moments[span_start:span_end], mix_weight[level]) for level, (span_start, span_end) in enumerate(LEVEL_SPANS)]
    scalar = mixed_out[0][0]
    gating = jax.nn.sigmoid(scalar)
    gate_slope = gating * (1.0 - gating)
    cot_float = cotangent.astype(jnp.float32)
    higher = jnp.concatenate(mixed_out[1:], 0)
    first_term = cot_float[0] * (gating + scalar * gate_slope) + lax.optimization_barrier(jnp.sum(cot_float[1:] * higher, 0)) * gate_slope
    dmixed = jnp.concatenate([first_term[None], cot_float[1:] * gating[None]], 0).astype(jnp.bfloat16)
    dmoments = jnp.concatenate([product('mpd,cd->mpc', dmixed[span_start:span_end], mix_weight[level]) for level, (span_start, span_end) in enumerate(LEVEL_SPANS)], 0).astype(jnp.bfloat16)
    mix_part = jnp.stack([product('mpc,mpd->cd', moments[span_start:span_end], dmixed[span_start:span_end]) for span_start, span_end in LEVEL_SPANS])
    return (dmoments, mix_part)

def reference(cotangent, displacement, neighbours, counts, atom_feat, radial_weight, mix_weight):
    nbrick = GROUPS * BRICKS
    channels = atom_feat.shape[3]
    nbasis = radial_weight.shape[1]
    atom_table = atom_feat.reshape(nbrick * A_DEV, channels)
    brick_ids = jnp.arange(nbrick).astype(jnp.int32)

    def per_brick(carry, inputs):
        grads, radial_acc, mix_acc = carry
        brick, cot_brick, disp_brick, nbr_brick, count_brick = inputs
        group_id = brick // BRICKS
        column_id = brick % BRICKS
        slot_id = nbr_brick // A_DEV
        local_id = nbr_brick % A_DEV
        group_of = (group_id + slot_id // 3 - 1 + GROUPS) % GROUPS
        column_of = (column_id + slot_id % 3 - 1 + BRICKS) % BRICKS
        global_id = ((group_of * BRICKS + column_of) * A_DEV + local_id).astype(jnp.int32)
        filled_slots = (lax.broadcasted_iota(jnp.int32, nbr_brick.shape, 0) < count_brick[None]).astype(jnp.float32)
        angular = harmonics(disp_brick) * filled_slots[None]
        radial_basis = basis(disp_brick, nbasis)
        radial = product('bkp,lbc->lkpc', radial_basis, radial_weight)
        features = atom_table[global_id].astype(jnp.float32)
        moments = jnp.concatenate([product('mkp,kpc->mpc', angular[span_start:span_end], radial[level] * features) for level, (span_start, span_end) in enumerate(LEVEL_SPANS)], 0).astype(jnp.bfloat16)
        dmoments, mix_part = gate_backward(moments, mix_weight, cot_brick)
        contrib = jnp.zeros(features.shape, jnp.float32)
        radial_parts = []
        for level, (span_start, span_end) in enumerate(LEVEL_SPANS):
            traced = product('mkp,mpc->kpc', angular[span_start:span_end], dmoments[span_start:span_end])
            contrib = contrib + radial[level] * traced
            radial_parts.append(product('bkp,kpc->bc', radial_basis, features * traced))
        grads = grads.at[global_id.reshape(-1)].add(contrib.reshape(-1, channels))
        return ((grads, radial_acc + jnp.stack(radial_parts), mix_acc + mix_part), None)
    start = (jnp.zeros((nbrick * A_DEV, channels), jnp.float32), jnp.zeros(radial_weight.shape, jnp.float32), jnp.zeros(mix_weight.shape, jnp.float32))
    inputs = (brick_ids, cotangent.reshape((nbrick,) + cotangent.shape[2:]), displacement.reshape((nbrick,) + displacement.shape[2:]), neighbours.reshape((nbrick,) + neighbours.shape[2:]), counts.reshape((nbrick,) + counts.shape[2:]))
    (grads, radial_grad, mix_grad), _ = lax.scan(per_brick, start, inputs)
    return (grads.reshape(atom_feat.shape), radial_grad, mix_grad)
```

```python
import functools
import math

import jax
import jax.numpy as jnp
from jax import lax
from jax.experimental import pallas as pl
from jax.experimental.pallas import tpu as pltpu
from jax.sharding import PartitionSpec as P

CUTOFF = 4.0
LEVEL_SPANS = ((0, 1), (1, 4), (4, 9))
LEVEL_OF = (0, 1, 1, 1, 2, 2, 2, 2, 2)
ORDER = (0, 1, 2, 6, 7, 8, 3, 5, 4)
MESH = pl.DeviceIdType.MESH
TILE = 16
NT = (((1,), (1,)), ((), ()))
F32 = jnp.float32
BF16 = jnp.bfloat16


def dot(a, b):
    return jnp.dot(a, b, preferred_element_type=F32)


def dot_nt(a, b):
    return lax.dot_general(a, b, NT, preferred_element_type=F32)


def kernel(
    ngz, nxy,
    cot_ref, disp_ref, nbr_ref, cnt_ref, atom_ref, rw_ref, mw_ref,
    agrad_ref, rgrad_ref, mgrad_ref,
    tbl, oh, key, half, ang, dist, env, basis, wpad, wt, radial, feat, cott, mixt,
    mom, dmom, ft, con, gsend, grecv, mixp, mixrs, mixgz, radgz, radxy,
    halo_s, halo_r, back_s, back_r, mrs_s, mrs_r, mgz_s, mgz_r, mag_s, mag_r,
    rgz_s, rgz_r, rxy_s, rxy_r,
):
    g = lax.axis_index("gz")
    b = lax.axis_index("xy")
    nk, npr = nbr_ref.shape[2], nbr_ref.shape[3]
    ch = atom_ref.shape[3]
    hb = atom_ref.shape[2] // 2
    nb = rw_ref.shape[1]
    rows = ch // nxy

    def at(dg, db):
        return (lax.rem(g + dg + ngz, ngz), lax.rem(b + db + nxy, nxy))

    barrier = pltpu.get_barrier_semaphore()
    peers = [(0, d) for d in range(1, nxy)] + [(d, 0) for d in range(1, ngz)]
    peers += [(-1, -1), (-1, 1), (1, -1), (1, 1)]
    for dg, db in peers:
        pl.semaphore_signal(barrier, inc=1, device_id=at(dg, db), device_id_type=MESH)

    own = pl.ds(8 * hb, hb)
    for h in range(2):
        tbl[h * ch:(h + 1) * ch, own] = (
            atom_ref[0, 0, h * hb:(h + 1) * hb, :].astype(F32).T.astype(BF16)
        )
    pl.semaphore_wait(barrier, len(peers))

    halo = []
    for pos in range(8):
        s = ORDER[pos]
        dg, db = s // 3 - 1, s % 3 - 1
        halo.append(pltpu.make_async_remote_copy(
            src_ref=tbl.at[:, own], dst_ref=tbl.at[:, pl.ds(pos * hb, hb)],
            send_sem=halo_s.at[pos], recv_sem=halo_r.at[pos],
            device_id=at(-dg, -db), device_id_type=MESH))
    for c in halo:
        c.start()

    n = nbr_ref[0, 0]
    low = lax.bitwise_and(n, hb - 1)
    slot = lax.shift_right_logical(n, int(math.log2(2 * hb)))
    for pos in range(9):
        key[pos] = jnp.where(slot == ORDER[pos], low, -1).astype(F32)
    half[...] = lax.bitwise_and(n, hb)
    x = disp_ref[0, 0, 0] * (1.0 / CUTOFF)
    y = disp_ref[0, 0, 1] * (1.0 / CUTOFF)
    z = disp_ref[0, 0, 2] * (1.0 / CUTOFF)
    mask = (lax.broadcasted_iota(jnp.int32, (nk, npr), 0) < cnt_ref[0]).astype(F32)
    r3, r5, r15 = math.sqrt(3.0), math.sqrt(5.0), math.sqrt(15.0)
    comps = (
        None, r3 * x, r3 * y, r3 * z, r15 * x * y, r15 * y * z,
        0.5 * r5 * (2.0 * z * z - x * x - y * y), r15 * x * z, 0.5 * r15 * (x * x - y * y),
    )
    for m in range(9):
        ang[m] = mask if m == 0 else comps[m] * mask
    d0, d1, d2 = disp_ref[0, 0, 0], disp_ref[0, 0, 1], disp_ref[0, 0, 2]
    r = jnp.sqrt(d0 * d0 + d1 * d1 + d2 * d2)
    dist[...] = r
    env[...] = 0.5 * (jnp.cos(r * (math.pi / CUTOFF)) + 1.0)

    wpad[...] = jnp.zeros(wpad.shape, F32)
    for l in range(3):
        w = rw_ref[l]
        hi = w.astype(BF16).astype(F32)
        lanes = slice(l * ch, (l + 1) * ch)
        wpad[0:nb, lanes] = hi
        wpad[nb:2 * nb, lanes] = w - hi
        wpad[2 * nb:3 * nb, lanes] = hi
        wt[lanes, :] = wpad[:, lanes].T.astype(BF16)
        mixt[l] = mw_ref[l].astype(F32).T.astype(BF16)
    for m in range(9):
        cott[m] = cot_ref[0, 0, m].astype(F32).T

    step = CUTOFF / (nb - 1)
    sharp = ((nb - 1) / CUTOFF) ** 2
    centres = lax.broadcasted_iota(jnp.int32, (nb, npr), 0).astype(F32) * step
    lines = lax.broadcasted_iota(jnp.int32, (hb, npr), 0).astype(F32).astype(BF16)
    one = jnp.ones((hb, npr), BF16)
    zero = jnp.zeros((hb, npr), BF16)

    def lanes_of(k, count=1):
        return pl.ds(pl.multiple_of(k * npr, npr), count * npr)

    def prepare(c, carry):
        for j in range(2):
            k = c * 2 + j
            at_k = lanes_of(k)
            off = dist[pl.ds(k, 1), :] - centres
            shaped = jnp.exp(-sharp * (off * off)) * env[pl.ds(k, 1), :]
            hi = shaped.astype(BF16)
            basis[0:nb, at_k] = hi
            basis[nb:2 * nb, at_k] = hi
            basis[2 * nb:3 * nb, at_k] = (shaped - hi.astype(F32)).astype(BF16)
            for pos in range(9):
                row = jnp.broadcast_to(key[pos, pl.ds(k, 1), :], (hb, npr)).astype(BF16)
                oh[pos * hb:(pos + 1) * hb, at_k] = jnp.where(lines == row, one, zero)
        rad = dot(wt[:, 0:3 * nb], basis[:, lanes_of(c * 2, 2)])
        for j in range(2):
            radial[c * 2 + j] = rad[:, j * npr:(j + 1) * npr]
        return carry

    lax.fori_loop(0, nk // 2, prepare, 0)

    for c in halo:
        c.wait_recv()

    def gather(c, carry):
        both = dot(tbl[...], oh[:, lanes_of(c * 2, 2)])
        for j in range(2):
            k = c * 2 + j
            cols = slice(j * npr, (j + 1) * npr)
            upper = half[pl.ds(k, 1), :] > 0
            feat[k] = jnp.where(upper, both[ch:, cols], both[:ch, cols])
        return carry

    lax.fori_loop(0, nk // 2, gather, 0)

    def moment_tile(t, carry):
        at_t = pl.ds(pl.multiple_of(t * TILE, TILE), TILE)

        def body(k, acc):
            f = feat[k, at_t, :]
            w = [
                radial[k, pl.ds(pl.multiple_of(l * ch + t * TILE, TILE), TILE), :] * f
                for l in range(3)
            ]
            return tuple(
                acc[m] + ang[m, pl.ds(k, 1), :] * w[LEVEL_OF[m]] for m in range(9)
            )

        acc = lax.fori_loop(0, nk, body, tuple(jnp.zeros((TILE, npr), F32) for _ in range(9)),
                            unroll=4)
        for m in range(9):
            mom[at_t, m * npr:(m + 1) * npr] = acc[m].astype(BF16)
        return carry

    lax.fori_loop(0, ch // TILE, moment_tile, 0)

    scalar = dot(mixt[0], mom[:, 0:npr])
    gating = jax.nn.sigmoid(scalar)
    slope = gating * (1.0 - gating)
    inner = jnp.zeros((ch, npr), F32)
    dmx = [None] * 9
    for m in range(1, 9):
        inner = inner + cott[m] * dot(mixt[LEVEL_OF[m]], mom[:, m * npr:(m + 1) * npr])
        dmx[m] = (cott[m] * gating).astype(BF16)
    dmx[0] = (cott[0] * (gating + scalar * slope) + inner * slope).astype(BF16)
    for l, (lo, hi) in enumerate(LEVEL_SPANS):
        total = None
        for m in range(lo, hi):
            part = dot_nt(mom[:, m * npr:(m + 1) * npr], dmx[m])
            total = part if total is None else total + part
        mixp[l] = total

    mixrs[b] = mixp[:, pl.ds(pl.multiple_of(b * rows, rows), rows), :]
    mrs = []
    for d in range(1, nxy):
        to = lax.rem(b + d, nxy)
        mrs.append(pltpu.make_async_remote_copy(
            src_ref=mixp.at[:, pl.ds(pl.multiple_of(to * rows, rows), rows), :],
            dst_ref=mixrs.at[b],
            send_sem=mrs_s.at[d], recv_sem=mrs_r.at[d],
            device_id=(g, to), device_id_type=MESH))
    for c in mrs:
        c.start()

    for m in range(9):
        dmom[m] = dot(mw_ref[LEVEL_OF[m]], dmx[m]).astype(BF16).astype(F32)

    def trace_tile(t, carry):
        at_t = pl.ds(pl.multiple_of(t * TILE, TILE), TILE)
        dm = [dmom[m, at_t, :] for m in range(9)]

        def body(k, carry):
            f = feat[k, at_t, :]
            at_k = lanes_of(k)
            total = None
            for l, (lo, hi) in enumerate(LEVEL_SPANS):
                tr = None
                for m in range(lo, hi):
                    part = ang[m, pl.ds(k, 1), :] * dm[m]
                    tr = part if tr is None else tr + part
                at_l = pl.ds(pl.multiple_of(l * ch + t * TILE, TILE), TILE)
                part = radial[k, at_l, :] * tr
                total = part if total is None else total + part
                ft[at_l, at_k] = (f * tr).astype(BF16)
            upper = half[pl.ds(k, 1), :] > 0
            con[at_t, at_k] = jnp.where(upper, 0.0, total).astype(BF16)
            con[pl.ds(pl.multiple_of(ch + t * TILE, TILE), TILE), at_k] = (
                jnp.where(upper, total, 0.0).astype(BF16)
            )
            return carry

        return lax.fori_loop(0, nk, body, carry, unroll=4)

    lax.fori_loop(0, ch // TILE, trace_tile, 0)

    rad = dot_nt(basis[...], ft[...])
    rad = rad[0:nb] + rad[2 * nb:3 * nb]
    for l in range(3):
        radgz[g, l] = rad[:, l * ch:(l + 1) * ch]
    rgz = []
    for d in range(1, ngz):
        rgz.append(pltpu.make_async_remote_copy(
            src_ref=radgz.at[g], dst_ref=radgz.at[g],
            send_sem=rgz_s.at[d], recv_sem=rgz_r.at[d],
            device_id=at(d, 0), device_id_type=MESH))
    for c in rgz:
        c.start()

    for c in mrs:
        c.wait_recv()
    total = mixrs[0]
    for i in range(1, nxy):
        total = total + mixrs[i]
    mixgz[g] = total
    mgz = []
    for d in range(1, ngz):
        mgz.append(pltpu.make_async_remote_copy(
            src_ref=mixgz.at[g], dst_ref=mixgz.at[g],
            send_sem=mgz_s.at[d], recv_sem=mgz_r.at[d],
            device_id=at(d, 0), device_id_type=MESH))
    for c in mgz:
        c.start()

    back = []

    def scatter(first, last):
        res = dot_nt(oh[first * hb:last * hb, :], con[...])
        for pos in range(first, last):
            block = res[(pos - first) * hb:(pos - first + 1) * hb]
            gsend[pos, 0:hb] = block[:, :ch].astype(BF16)
            gsend[pos, hb:2 * hb] = block[:, ch:].astype(BF16)
            s = ORDER[pos]
            copy = pltpu.make_async_remote_copy(
                src_ref=gsend.at[pos], dst_ref=grecv.at[pos],
                send_sem=back_s.at[pos], recv_sem=back_r.at[pos],
                device_id=at(s // 3 - 1, s % 3 - 1), device_id_type=MESH)
            copy.start()
            back.append(copy)

    scatter(0, 3)

    for c in rgz:
        c.wait_recv()
    total = radgz[0]
    for i in range(1, ngz):
        total = total + radgz[i]
    radxy[b] = total
    rxy = []
    for d in range(1, nxy):
        rxy.append(pltpu.make_async_remote_copy(
            src_ref=radxy.at[b], dst_ref=radxy.at[b],
            send_sem=rxy_s.at[d], recv_sem=rxy_r.at[d],
            device_id=at(0, d), device_id_type=MESH))
    for c in rxy:
        c.start()

    scatter(3, 6)

    for c in mgz:
        c.wait_recv()
    total = mixgz[0]
    for i in range(1, ngz):
        total = total + mixgz[i]
    mine = pl.ds(pl.multiple_of(b * rows, rows), rows)
    mgrad_ref[:, mine, :] = total
    mag = []
    for d in range(1, nxy):
        mag.append(pltpu.make_async_remote_copy(
            src_ref=mgrad_ref.at[:, mine, :], dst_ref=mgrad_ref.at[:, mine, :],
            send_sem=mag_s.at[d], recv_sem=mag_r.at[d],
            device_id=at(0, d), device_id_type=MESH))
    for c in mag:
        c.start()

    scatter(6, 8)
    kept = dot_nt(oh[8 * hb:9 * hb, :], con[...])
    agrad_ref[0, 0, 0:hb] = kept[:, :ch]
    agrad_ref[0, 0, hb:2 * hb] = kept[:, ch:]

    for c in rxy:
        c.wait_recv()
    total = radxy[0]
    for i in range(1, nxy):
        total = total + radxy[i]
    rgrad_ref[...] = total

    for c in back:
        c.wait_recv()
    for h in range(2):
        part = agrad_ref[0, 0, h * hb:(h + 1) * hb]
        for pos in range(8):
            part = part + grecv[pos, h * hb:(h + 1) * hb].astype(F32)
        agrad_ref[0, 0, h * hb:(h + 1) * hb] = part
    for c in mag:
        c.wait_recv()
    for c in halo + mrs + rgz + mgz + back + rxy + mag:
        c.wait_send()


def shards(cotangent, displacement, neighbours, counts, atom_feat, radial_weight, mix_weight):
    ngz, nxy = lax.axis_size("gz"), lax.axis_size("xy")
    nk, npr = neighbours.shape[2:]
    natom, ch = atom_feat.shape[2:]
    nb = radial_weight.shape[1]
    hb = natom // 2
    slots = nk * npr
    rows = ch // nxy
    V = pltpu.VMEM
    dma = pltpu.SemaphoreType.DMA
    vm = pl.BlockSpec(memory_space=pltpu.VMEM)
    return pl.pallas_call(
        functools.partial(kernel, ngz, nxy),
        out_shape=(
            jax.ShapeDtypeStruct((1, 1, natom, ch), F32),
            jax.ShapeDtypeStruct((3, nb, ch), F32),
            jax.ShapeDtypeStruct((3, ch, ch), F32),
        ),
        in_specs=[vm] * 7,
        out_specs=(vm, vm, vm),
        scratch_shapes=[
            V((2 * ch, 9 * hb), BF16),
            V((9 * hb, slots), BF16),
            V((9, nk, npr), F32),
            V((nk, npr), jnp.int32),
            V((9, nk, npr), F32),
            V((nk, npr), F32),
            V((nk, npr), F32),
            V((3 * nb, slots), BF16),
            V((128, 3 * ch), F32),
            V((3 * ch, 128), BF16),
            V((nk, 3 * ch, npr), F32),
            V((nk, ch, npr), F32),
            V((9, ch, npr), F32),
            V((3, ch, ch), BF16),
            V((ch, 9 * npr), BF16),
            V((9, ch, npr), F32),
            V((3 * ch, slots), BF16),
            V((2 * ch, slots), BF16),
            V((8, natom, ch), BF16),
            V((8, natom, ch), BF16),
            V((3, ch, ch), F32),
            V((nxy, 3, rows, ch), F32),
            V((ngz, 3, rows, ch), F32),
            V((ngz, 3, nb, ch), F32),
            V((nxy, 3, nb, ch), F32),
            dma((8,)), dma((8,)), dma((8,)), dma((8,)),
            dma((nxy,)), dma((nxy,)), dma((ngz,)), dma((ngz,)), dma((nxy,)), dma((nxy,)),
            dma((ngz,)), dma((ngz,)), dma((nxy,)), dma((nxy,)),
        ],
        compiler_params=pltpu.CompilerParams(
            collective_id=0, has_side_effects=True, vmem_limit_bytes=48 * 1024 * 1024
        ),
    )(cotangent, displacement, neighbours, counts, atom_feat, radial_weight, mix_weight)


def solution(mesh):
    in_specs = (
        P("gz", "xy", None, None, None),
        P("gz", "xy", None, None, None),
        P("gz", "xy", None, None),
        P("gz", "xy", None),
        P("gz", "xy", None, None),
        P(),
        P(),
    )
    out_specs = (P("gz", "xy", None, None), P(), P())
    return jax.shard_map(shards, mesh=mesh, in_specs=in_specs, out_specs=out_specs, check_vma=False)
```

```python
import functools
import math

import jax
import jax.numpy as jnp
from jax import lax
from jax.experimental import pallas as pl
from jax.experimental.pallas import tpu as pltpu
from jax.sharding import PartitionSpec as P

CUTOFF = 4.0
LEVEL_SPANS = ((0, 1), (1, 4), (4, 9))
LEVEL_OF = (0, 1, 1, 1, 2, 2, 2, 2, 2)
ORDER = (0, 1, 2, 6, 7, 8, 3, 5, 4)
MESH = pl.DeviceIdType.MESH
TILE = 16
NT = (((1,), (1,)), ((), ()))
F32 = jnp.float32
BF16 = jnp.bfloat16


def dot(a, b):
    return jnp.dot(a, b, preferred_element_type=F32)


def dot_nt(a, b):
    return lax.dot_general(a, b, NT, preferred_element_type=F32)


def added(ref):
    total = ref[0].astype(F32)
    for i in range(1, ref.shape[0]):
        total = total + ref[i].astype(F32)
    return total


def kernel(
    ngz, nxy,
    cot_hbm, disp_hbm, nbr_hbm, cnt_hbm, atom_hbm, rw_hbm, mw_hbm,
    agrad_ref, rgrad_ref, mgrad_ref,
    tbl, oh, key, half, ang, dist, env, basis, wpad, wt, radial, feat, cott, mixt,
    mom, dmom, ft, con, gsend, grecv, mixp, mixrs, mixgz, mixag, radgz, radxy,
    halo_s, halo_r, back_s, back_r, mrs_s, mrs_r, mgz_s, mgz_r, mag_s, mag_r,
    rgz_s, rgz_r, rxy_s, rxy_r,
    atom_ref, nbr_ref, disp_ref, cnt_ref, rw_ref, mw_ref, cot_ref, load_s,
):
    g = lax.axis_index("gz")
    b = lax.axis_index("xy")
    nk, npr = nbr_ref.shape[2], nbr_ref.shape[3]
    ch = atom_ref.shape[3]
    hb = atom_ref.shape[2] // 2
    nb = rw_ref.shape[1]
    rows = ch // nxy

    def at(dg, db):
        return (lax.rem(g + dg + ngz, ngz), lax.rem(b + db + nxy, nxy))

    loads = [
        pltpu.make_async_copy(src, dst, load_s.at[i])
        for i, (src, dst) in enumerate((
            (atom_hbm, atom_ref), (nbr_hbm, nbr_ref), (disp_hbm, disp_ref), (cnt_hbm, cnt_ref),
            (rw_hbm, rw_ref), (mw_hbm, mw_ref), (cot_hbm, cot_ref),
        ))
    ]
    for c in loads:
        c.start()

    barrier = pltpu.get_barrier_semaphore()
    peers = [(0, d) for d in range(1, nxy)] + [(d, 0) for d in range(1, ngz)]
    peers += [(-1, -1), (-1, 1), (1, -1), (1, 1)]
    for dg, db in peers:
        pl.semaphore_signal(barrier, inc=1, device_id=at(dg, db), device_id_type=MESH)

    own = pl.ds(8 * hb, hb)
    loads[0].wait()
    for h in range(2):
        tbl[h * ch:(h + 1) * ch, own] = (
            atom_ref[0, 0, h * hb:(h + 1) * hb, :].astype(F32).T.astype(BF16)
        )
    pl.semaphore_wait(barrier, len(peers))

    halo = []
    for pos in range(8):
        s = ORDER[pos]
        dg, db = s // 3 - 1, s % 3 - 1
        halo.append(pltpu.make_async_remote_copy(
            src_ref=tbl.at[:, own], dst_ref=tbl.at[:, pl.ds(pos * hb, hb)],
            send_sem=halo_s.at[pos], recv_sem=halo_r.at[pos],
            device_id=at(-dg, -db), device_id_type=MESH))
    for c in halo:
        c.start()

    for c in loads[1:]:
        c.wait()
    n = nbr_ref[0, 0]
    low = lax.bitwise_and(n, hb - 1)
    slot = lax.shift_right_logical(n, int(math.log2(2 * hb)))
    for pos in range(9):
        key[pos] = jnp.where(slot == ORDER[pos], low, -1).astype(F32)
    half[...] = lax.bitwise_and(n, hb)
    x = disp_ref[0, 0, 0] * (1.0 / CUTOFF)
    y = disp_ref[0, 0, 1] * (1.0 / CUTOFF)
    z = disp_ref[0, 0, 2] * (1.0 / CUTOFF)
    mask = (lax.broadcasted_iota(jnp.int32, (nk, npr), 0) < cnt_ref[0]).astype(F32)
    r3, r5, r15 = math.sqrt(3.0), math.sqrt(5.0), math.sqrt(15.0)
    comps = (
        None, r3 * x, r3 * y, r3 * z, r15 * x * y, r15 * y * z,
        0.5 * r5 * (2.0 * z * z - x * x - y * y), r15 * x * z, 0.5 * r15 * (x * x - y * y),
    )
    for m in range(9):
        ang[m] = mask if m == 0 else comps[m] * mask
    d0, d1, d2 = disp_ref[0, 0, 0], disp_ref[0, 0, 1], disp_ref[0, 0, 2]
    r = jnp.sqrt(d0 * d0 + d1 * d1 + d2 * d2)
    dist[...] = r
    env[...] = 0.5 * (jnp.cos(r * (math.pi / CUTOFF)) + 1.0)

    wpad[...] = jnp.zeros(wpad.shape, F32)
    for l in range(3):
        w = rw_ref[l]
        hi = w.astype(BF16).astype(F32)
        lanes = slice(l * ch, (l + 1) * ch)
        wpad[0:nb, lanes] = hi
        wpad[nb:2 * nb, lanes] = w - hi
        wpad[2 * nb:3 * nb, lanes] = hi
        wt[lanes, :] = wpad[:, lanes].T.astype(BF16)
        mixt[l] = mw_ref[l].astype(F32).T.astype(BF16)
    for m in range(9):
        cott[m] = cot_ref[0, 0, m].astype(F32).T

    step = CUTOFF / (nb - 1)
    sharp = ((nb - 1) / CUTOFF) ** 2
    centres = lax.broadcasted_iota(jnp.int32, (nb, npr), 0).astype(F32) * step
    lines = lax.broadcasted_iota(jnp.int32, (hb, npr), 0).astype(F32).astype(BF16)
    one = jnp.ones((hb, npr), BF16)
    zero = jnp.zeros((hb, npr), BF16)

    def lanes_of(k, count=1):
        return pl.ds(pl.multiple_of(k * npr, npr), count * npr)

    def prepare(c, carry):
        for j in range(2):
            k = c * 2 + j
            at_k = lanes_of(k)
            off = dist[pl.ds(k, 1), :] - centres
            shaped = jnp.exp(-sharp * (off * off)) * env[pl.ds(k, 1), :]
            hi = shaped.astype(BF16)
            basis[0:nb, at_k] = hi
            basis[nb:2 * nb, at_k] = hi
            basis[2 * nb:3 * nb, at_k] = (shaped - hi.astype(F32)).astype(BF16)
            for pos in range(9):
                row = jnp.broadcast_to(key[pos, pl.ds(k, 1), :], (hb, npr)).astype(BF16)
                oh[pos * hb:(pos + 1) * hb, at_k] = jnp.where(lines == row, one, zero)
        rad = dot(wt[:, 0:3 * nb], basis[:, lanes_of(c * 2, 2)])
        for j in range(2):
            radial[c * 2 + j] = rad[:, j * npr:(j + 1) * npr]
        return carry

    lax.fori_loop(0, nk // 2, prepare, 0)

    for c in halo:
        c.wait_recv()

    def gather(c, carry):
        both = dot(tbl[...], oh[:, lanes_of(c * 2, 2)])
        for j in range(2):
            k = c * 2 + j
            cols = slice(j * npr, (j + 1) * npr)
            upper = half[pl.ds(k, 1), :] > 0
            feat[k] = jnp.where(upper, both[ch:, cols], both[:ch, cols])
        return carry

    lax.fori_loop(0, nk // 2, gather, 0)

    def moment_tile(t, carry):
        at_t = pl.ds(pl.multiple_of(t * TILE, TILE), TILE)

        def body(k, acc):
            f = feat[k, at_t, :]
            w = [
                radial[k, pl.ds(pl.multiple_of(l * ch + t * TILE, TILE), TILE), :] * f
                for l in range(3)
            ]
            return tuple(
                acc[m] + ang[m, pl.ds(k, 1), :] * w[LEVEL_OF[m]] for m in range(9)
            )

        acc = lax.fori_loop(0, nk, body, tuple(jnp.zeros((TILE, npr), F32) for _ in range(9)),
                            unroll=4)
        for m in range(9):
            mom[at_t, m * npr:(m + 1) * npr] = acc[m].astype(BF16)
        return carry

    lax.fori_loop(0, ch // TILE, moment_tile, 0)

    scalar = dot(mixt[0], mom[:, 0:npr])
    gating = jax.nn.sigmoid(scalar)
    slope = gating * (1.0 - gating)
    inner = jnp.zeros((ch, npr), F32)
    dmx = [None] * 9
    for m in range(1, 9):
        inner = inner + cott[m] * dot(mixt[LEVEL_OF[m]], mom[:, m * npr:(m + 1) * npr])
        dmx[m] = (cott[m] * gating).astype(BF16)
    dmx[0] = (cott[0] * (gating + scalar * slope) + inner * slope).astype(BF16)
    for l, (lo, hi) in enumerate(LEVEL_SPANS):
        total = None
        for m in range(lo, hi):
            part = dot_nt(mom[:, m * npr:(m + 1) * npr], dmx[m])
            total = part if total is None else total + part
        for i in range(nxy):
            mixp[i, l] = total[i * rows:(i + 1) * rows].astype(mixp.dtype)

    mixrs[b] = mixp[b]
    mrs = []
    for d in range(1, nxy):
        to = lax.rem(b + d, nxy)
        mrs.append(pltpu.make_async_remote_copy(
            src_ref=mixp.at[to],
            dst_ref=mixrs.at[b],
            send_sem=mrs_s.at[d], recv_sem=mrs_r.at[d],
            device_id=(g, to), device_id_type=MESH))
    for c in mrs:
        c.start()

    for m in range(9):
        dmom[m] = dot(mw_ref[LEVEL_OF[m]], dmx[m]).astype(BF16).astype(F32)

    def trace_tile(t, carry):
        at_t = pl.ds(pl.multiple_of(t * TILE, TILE), TILE)
        dm = [dmom[m, at_t, :] for m in range(9)]

        def body(k, carry):
            f = feat[k, at_t, :]
            at_k = lanes_of(k)
            total = None
            for l, (lo, hi) in enumerate(LEVEL_SPANS):
                tr = None
                for m in range(lo, hi):
                    part = ang[m, pl.ds(k, 1), :] * dm[m]
                    tr = part if tr is None else tr + part
                at_l = pl.ds(pl.multiple_of(l * ch + t * TILE, TILE), TILE)
                part = radial[k, at_l, :] * tr
                total = part if total is None else total + part
                ft[at_l, at_k] = (f * tr).astype(BF16)
            upper = half[pl.ds(k, 1), :] > 0
            con[at_t, at_k] = jnp.where(upper, 0.0, total).astype(BF16)
            con[pl.ds(pl.multiple_of(ch + t * TILE, TILE), TILE), at_k] = (
                jnp.where(upper, total, 0.0).astype(BF16)
            )
            return carry

        return lax.fori_loop(0, nk, body, carry, unroll=4)

    lax.fori_loop(0, ch // TILE, trace_tile, 0)

    rad = dot_nt(basis[...], ft[...])
    rad = rad[0:nb] + rad[2 * nb:3 * nb]
    for l in range(3):
        radgz[g, l] = rad[:, l * ch:(l + 1) * ch].astype(BF16)
    rgz = []
    for d in range(1, ngz):
        rgz.append(pltpu.make_async_remote_copy(
            src_ref=radgz.at[g], dst_ref=radgz.at[g],
            send_sem=rgz_s.at[d], recv_sem=rgz_r.at[d],
            device_id=at(d, 0), device_id_type=MESH))
    for c in rgz:
        c.start()

    for c in mrs:
        c.wait_recv()
    mixgz[g] = added(mixrs).astype(mixgz.dtype)
    mgz = []
    for d in range(1, ngz):
        mgz.append(pltpu.make_async_remote_copy(
            src_ref=mixgz.at[g], dst_ref=mixgz.at[g],
            send_sem=mgz_s.at[d], recv_sem=mgz_r.at[d],
            device_id=at(d, 0), device_id_type=MESH))
    for c in mgz:
        c.start()

    back = []

    def scatter(first, last):
        res = dot_nt(oh[first * hb:last * hb, :], con[...])
        for pos in range(first, last):
            block = res[(pos - first) * hb:(pos - first + 1) * hb]
            gsend[pos, 0:hb] = block[:, :ch].astype(BF16)
            gsend[pos, hb:2 * hb] = block[:, ch:].astype(BF16)
            s = ORDER[pos]
            copy = pltpu.make_async_remote_copy(
                src_ref=gsend.at[pos], dst_ref=grecv.at[pos],
                send_sem=back_s.at[pos], recv_sem=back_r.at[pos],
                device_id=at(s // 3 - 1, s % 3 - 1), device_id_type=MESH)
            copy.start()
            back.append(copy)

    scatter(0, 3)

    for c in rgz:
        c.wait_recv()
    radxy[b] = added(radgz).astype(BF16)
    rxy = []
    for d in range(1, nxy):
        rxy.append(pltpu.make_async_remote_copy(
            src_ref=radxy.at[b], dst_ref=radxy.at[b],
            send_sem=rxy_s.at[d], recv_sem=rxy_r.at[d],
            device_id=at(0, d), device_id_type=MESH))
    for c in rxy:
        c.start()

    scatter(3, 6)

    for c in mgz:
        c.wait_recv()
    mixag[b] = added(mixgz).astype(mixag.dtype)
    mag = []
    for d in range(1, nxy):
        mag.append(pltpu.make_async_remote_copy(
            src_ref=mixag.at[b], dst_ref=mixag.at[b],
            send_sem=mag_s.at[d], recv_sem=mag_r.at[d],
            device_id=at(0, d), device_id_type=MESH))
    for c in mag:
        c.start()

    scatter(6, 8)
    kept = dot_nt(oh[8 * hb:9 * hb, :], con[...])
    agrad_ref[0, 0, 0:hb] = kept[:, :ch]
    agrad_ref[0, 0, hb:2 * hb] = kept[:, ch:]

    for c in rxy:
        c.wait_recv()
    rgrad_ref[...] = added(radxy)

    for c in back:
        c.wait_recv()
    for h in range(2):
        part = agrad_ref[0, 0, h * hb:(h + 1) * hb]
        for pos in range(8):
            part = part + grecv[pos, h * hb:(h + 1) * hb].astype(F32)
        agrad_ref[0, 0, h * hb:(h + 1) * hb] = part
    for c in mag:
        c.wait_recv()
    for i in range(nxy):
        mgrad_ref[:, i * rows:(i + 1) * rows, :] = mixag[i].astype(F32)
    for c in halo + mrs + rgz + mgz + back + rxy + mag:
        c.wait_send()


def shards(cotangent, displacement, neighbours, counts, atom_feat, radial_weight, mix_weight):
    ngz, nxy = lax.axis_size("gz"), lax.axis_size("xy")
    nk, npr = neighbours.shape[2:]
    natom, ch = atom_feat.shape[2:]
    nb = radial_weight.shape[1]
    hb = natom // 2
    slots = nk * npr
    rows = ch // nxy
    sent = F32 if rows % 16 else BF16
    V = pltpu.VMEM
    dma = pltpu.SemaphoreType.DMA
    vm = pl.BlockSpec(memory_space=pltpu.VMEM)
    return pl.pallas_call(
        functools.partial(kernel, ngz, nxy),
        out_shape=(
            jax.ShapeDtypeStruct((1, 1, natom, ch), F32),
            jax.ShapeDtypeStruct((3, nb, ch), F32),
            jax.ShapeDtypeStruct((3, ch, ch), F32),
        ),
        in_specs=[pl.BlockSpec(memory_space=pl.ANY)] * 7,
        out_specs=(vm, vm, vm),
        scratch_shapes=[
            V((2 * ch, 9 * hb), BF16),
            V((9 * hb, slots), BF16),
            V((9, nk, npr), F32),
            V((nk, npr), jnp.int32),
            V((9, nk, npr), F32),
            V((nk, npr), F32),
            V((nk, npr), F32),
            V((3 * nb, slots), BF16),
            V((128, 3 * ch), F32),
            V((3 * ch, 128), BF16),
            V((nk, 3 * ch, npr), F32),
            V((nk, ch, npr), F32),
            V((9, ch, npr), F32),
            V((3, ch, ch), BF16),
            V((ch, 9 * npr), BF16),
            V((9, ch, npr), F32),
            V((3 * ch, slots), BF16),
            V((2 * ch, slots), BF16),
            V((8, natom, ch), BF16),
            V((8, natom, ch), BF16),
            V((nxy, 3, rows, ch), sent),
            V((nxy, 3, rows, ch), sent),
            V((ngz, 3, rows, ch), sent),
            V((nxy, 3, rows, ch), sent),
            V((ngz, 3, nb, ch), BF16),
            V((nxy, 3, nb, ch), BF16),
            dma((8,)), dma((8,)), dma((8,)), dma((8,)),
            dma((nxy,)), dma((nxy,)), dma((ngz,)), dma((ngz,)), dma((nxy,)), dma((nxy,)),
            dma((ngz,)), dma((ngz,)), dma((nxy,)), dma((nxy,)),
            V(atom_feat.shape, BF16), V(neighbours.shape, jnp.int32), V(displacement.shape, F32),
            V(counts.shape, jnp.int32), V(radial_weight.shape, F32), V(mix_weight.shape, BF16),
            V(cotangent.shape, BF16), dma((7,)),
        ],
        compiler_params=pltpu.CompilerParams(
            collective_id=0, has_side_effects=True, vmem_limit_bytes=48 * 1024 * 1024
        ),
    )(cotangent, displacement, neighbours, counts, atom_feat, radial_weight, mix_weight)


def solution(mesh):
    in_specs = (
        P("gz", "xy", None, None, None),
        P("gz", "xy", None, None, None),
        P("gz", "xy", None, None),
        P("gz", "xy", None),
        P("gz", "xy", None, None),
        P(),
        P(),
    )
    out_specs = (P("gz", "xy", None, None), P(), P())
    return jax.shard_map(shards, mesh=mesh, in_specs=in_specs, out_specs=out_specs, check_vma=False)
```

```python
import functools
import math

import jax
import jax.numpy as jnp
from jax import lax
from jax.experimental import pallas as pl
from jax.experimental.pallas import tpu as pltpu
from jax.sharding import PartitionSpec as P

CUTOFF = 4.0
LEVEL_SPANS = ((0, 1), (1, 4), (4, 9))
LEVEL_OF = (0, 1, 1, 1, 2, 2, 2, 2, 2)
ORDER = (0, 1, 2, 6, 7, 8, 3, 5, 4)
MESH = pl.DeviceIdType.MESH
TILE = 16
UNROLL = 4
PREP = 2
GATHER = 8
EARLY = 6
NT = (((1,), (1,)), ((), ()))
F32 = jnp.float32
BF16 = jnp.bfloat16


def dot(a, b):
    return jnp.dot(a, b, preferred_element_type=F32)


def dot_nt(a, b):
    return lax.dot_general(a, b, NT, preferred_element_type=F32)


def added(ref):
    total = ref[0].astype(F32)
    for i in range(1, ref.shape[0]):
        total = total + ref[i].astype(F32)
    return total


def kernel(
    ngz, nxy,
    cot_hbm, disp_hbm, nbr_hbm, cnt_hbm, atom_hbm, rw_hbm, mw_hbm,
    agrad_ref, rgrad_ref, mgrad_ref,
    tbl, oh, key, half, ang, dist, env, basis, wpad, wt, radial, feat, cott, mixt,
    mom, dmom, ft, con, gsend, grecv, mixp, mixrs, mixgz, mixag, radgz, radxy,
    halo_s, halo_r, back_s, back_r, mrs_s, mrs_r, mgz_s, mgz_r, mag_s, mag_r,
    rgz_s, rgz_r, rxy_s, rxy_r,
    atom_ref, nbr_ref, disp_ref, cnt_ref, rw_ref, mw_ref, cot_ref, load_s,
):
    g = lax.axis_index("gz")
    b = lax.axis_index("xy")
    nk, npr = nbr_ref.shape[2], nbr_ref.shape[3]
    ch = atom_ref.shape[3]
    hb = atom_ref.shape[2] // 2
    nb = rw_ref.shape[1]
    rows = ch // nxy

    def at(dg, db):
        return (lax.rem(g + dg + ngz, ngz), lax.rem(b + db + nxy, nxy))

    loads = [
        pltpu.make_async_copy(src, dst, load_s.at[i])
        for i, (src, dst) in enumerate((
            (atom_hbm, atom_ref), (nbr_hbm, nbr_ref), (disp_hbm, disp_ref), (cnt_hbm, cnt_ref),
            (rw_hbm, rw_ref), (mw_hbm, mw_ref), (cot_hbm, cot_ref),
        ))
    ]
    for c in loads:
        c.start()

    barrier = pltpu.get_barrier_semaphore()
    peers = [(0, d) for d in range(1, nxy)] + [(d, 0) for d in range(1, ngz)]
    peers += [(-1, -1), (-1, 1), (1, -1), (1, 1)]
    for dg, db in peers:
        pl.semaphore_signal(barrier, inc=1, device_id=at(dg, db), device_id_type=MESH)

    own = pl.ds(8 * hb, hb)
    loads[0].wait()
    for h in range(2):
        tbl[h * ch:(h + 1) * ch, own] = (
            atom_ref[0, 0, h * hb:(h + 1) * hb, :].astype(F32).T.astype(BF16)
        )
    for c in loads[1:]:
        c.wait()
    n = nbr_ref[0, 0]
    low = lax.bitwise_and(n, hb - 1)
    slot = lax.shift_right_logical(n, int(math.log2(2 * hb)))
    for pos in range(9):
        key[pos] = jnp.where(slot == ORDER[pos], low, -1).astype(F32)
    half[...] = lax.bitwise_and(n, hb)
    x = disp_ref[0, 0, 0] * (1.0 / CUTOFF)
    y = disp_ref[0, 0, 1] * (1.0 / CUTOFF)
    z = disp_ref[0, 0, 2] * (1.0 / CUTOFF)
    mask = (lax.broadcasted_iota(jnp.int32, (nk, npr), 0) < cnt_ref[0]).astype(F32)
    r3, r5, r15 = math.sqrt(3.0), math.sqrt(5.0), math.sqrt(15.0)
    comps = (
        None, r3 * x, r3 * y, r3 * z, r15 * x * y, r15 * y * z,
        0.5 * r5 * (2.0 * z * z - x * x - y * y), r15 * x * z, 0.5 * r15 * (x * x - y * y),
    )
    for m in range(9):
        ang[m] = mask if m == 0 else comps[m] * mask
    d0, d1, d2 = disp_ref[0, 0, 0], disp_ref[0, 0, 1], disp_ref[0, 0, 2]
    r = jnp.sqrt(d0 * d0 + d1 * d1 + d2 * d2)
    dist[...] = r
    env[...] = 0.5 * (jnp.cos(r * (math.pi / CUTOFF)) + 1.0)

    wpad[...] = jnp.zeros(wpad.shape, F32)
    for l in range(3):
        w = rw_ref[l]
        hi = w.astype(BF16).astype(F32)
        lanes = slice(l * ch, (l + 1) * ch)
        wpad[0:nb, lanes] = hi
        wpad[nb:2 * nb, lanes] = w - hi
        wpad[2 * nb:3 * nb, lanes] = hi
        wt[lanes, :] = wpad[:, lanes].T.astype(BF16)
        mixt[l] = mw_ref[l].astype(F32).T.astype(BF16)
    for m in range(9):
        cott[m] = cot_ref[0, 0, m].astype(F32).T

    step = CUTOFF / (nb - 1)
    sharp = ((nb - 1) / CUTOFF) ** 2
    centres = lax.broadcasted_iota(jnp.int32, (nb, npr), 0).astype(F32) * step
    lines = lax.broadcasted_iota(jnp.int32, (hb, npr), 0).astype(F32).astype(BF16)
    one = jnp.ones((hb, npr), BF16)
    zero = jnp.zeros((hb, npr), BF16)

    def lanes_of(k, count=1):
        return pl.ds(pl.multiple_of(k * npr, npr), count * npr)

    def prepare(c, carry):
        for j in range(PREP):
            k = c * PREP + j
            at_k = lanes_of(k)
            off = dist[pl.ds(k, 1), :] - centres
            shaped = jnp.exp(-sharp * (off * off)) * env[pl.ds(k, 1), :]
            hi = shaped.astype(BF16)
            basis[0:nb, at_k] = hi
            basis[nb:2 * nb, at_k] = hi
            basis[2 * nb:3 * nb, at_k] = (shaped - hi.astype(F32)).astype(BF16)
            for pos in range(9):
                row = jnp.broadcast_to(key[pos, pl.ds(k, 1), :], (hb, npr)).astype(BF16)
                oh[pos * hb:(pos + 1) * hb, at_k] = jnp.where(lines == row, one, zero)
        rad = dot(wt[:, 0:3 * nb], basis[:, lanes_of(c * PREP, PREP)])
        for j in range(PREP):
            radial[c * PREP + j] = rad[:, j * npr:(j + 1) * npr]
        return carry

    lax.fori_loop(0, EARLY, prepare, 0)

    pl.semaphore_wait(barrier, len(peers))

    halo = []
    for pos in range(8):
        s = ORDER[pos]
        dg, db = s // 3 - 1, s % 3 - 1
        halo.append(pltpu.make_async_remote_copy(
            src_ref=tbl.at[:, own], dst_ref=tbl.at[:, pl.ds(pos * hb, hb)],
            send_sem=halo_s.at[pos], recv_sem=halo_r.at[pos],
            device_id=at(-dg, -db), device_id_type=MESH))
    for c in halo:
        c.start()

    lax.fori_loop(EARLY, nk // PREP, prepare, 0)

    for c in halo:
        c.wait_recv()

    def gather(c, carry):
        both = dot(tbl[...], oh[:, lanes_of(c * GATHER, GATHER)])
        for j in range(GATHER):
            k = c * GATHER + j
            cols = slice(j * npr, (j + 1) * npr)
            upper = half[pl.ds(k, 1), :] > 0
            feat[k] = jnp.where(upper, both[ch:, cols], both[:ch, cols])
        return carry

    lax.fori_loop(0, nk // GATHER, gather, 0)

    def moment_tile(t, carry):
        at_t = pl.ds(pl.multiple_of(t * TILE, TILE), TILE)

        def body(k, acc):
            f = feat[k, at_t, :]
            w = [
                radial[k, pl.ds(pl.multiple_of(l * ch + t * TILE, TILE), TILE), :] * f
                for l in range(3)
            ]
            return tuple(
                acc[m] + ang[m, pl.ds(k, 1), :] * w[LEVEL_OF[m]] for m in range(9)
            )

        acc = lax.fori_loop(0, nk, body, tuple(jnp.zeros((TILE, npr), F32) for _ in range(9)),
                            unroll=UNROLL)
        for m in range(9):
            mom[at_t, m * npr:(m + 1) * npr] = acc[m].astype(BF16)
        return carry

    lax.fori_loop(0, ch // TILE, moment_tile, 0)

    scalar = dot(mixt[0], mom[:, 0:npr])
    gating = jax.nn.sigmoid(scalar)
    slope = gating * (1.0 - gating)
    inner = jnp.zeros((ch, npr), F32)
    dmx = [None] * 9
    for m in range(1, 9):
        inner = inner + cott[m] * dot(mixt[LEVEL_OF[m]], mom[:, m * npr:(m + 1) * npr])
        dmx[m] = (cott[m] * gating).astype(BF16)
    dmx[0] = (cott[0] * (gating + scalar * slope) + inner * slope).astype(BF16)
    for l, (lo, hi) in enumerate(LEVEL_SPANS):
        total = None
        for m in range(lo, hi):
            part = dot_nt(mom[:, m * npr:(m + 1) * npr], dmx[m])
            total = part if total is None else total + part
        for i in range(nxy):
            mixp[i, l] = total[i * rows:(i + 1) * rows].astype(mixp.dtype)

    mixrs[b] = mixp[b]
    mrs = []
    for d in range(1, nxy):
        to = lax.rem(b + d, nxy)
        mrs.append(pltpu.make_async_remote_copy(
            src_ref=mixp.at[to],
            dst_ref=mixrs.at[b],
            send_sem=mrs_s.at[d], recv_sem=mrs_r.at[d],
            device_id=(g, to), device_id_type=MESH))
    for c in mrs:
        c.start()

    for m in range(9):
        dmom[m] = dot(mw_ref[LEVEL_OF[m]], dmx[m]).astype(BF16).astype(F32)

    def trace_tile(t, carry):
        at_t = pl.ds(pl.multiple_of(t * TILE, TILE), TILE)
        dm = [dmom[m, at_t, :] for m in range(9)]

        def body(k, carry):
            f = feat[k, at_t, :]
            at_k = lanes_of(k)
            total = None
            for l, (lo, hi) in enumerate(LEVEL_SPANS):
                tr = None
                for m in range(lo, hi):
                    part = ang[m, pl.ds(k, 1), :] * dm[m]
                    tr = part if tr is None else tr + part
                at_l = pl.ds(pl.multiple_of(l * ch + t * TILE, TILE), TILE)
                part = radial[k, at_l, :] * tr
                total = part if total is None else total + part
                ft[at_l, at_k] = (f * tr).astype(BF16)
            upper = half[pl.ds(k, 1), :] > 0
            con[at_t, at_k] = jnp.where(upper, 0.0, total).astype(BF16)
            con[pl.ds(pl.multiple_of(ch + t * TILE, TILE), TILE), at_k] = (
                jnp.where(upper, total, 0.0).astype(BF16)
            )
            return carry

        return lax.fori_loop(0, nk, body, carry, unroll=UNROLL)

    lax.fori_loop(0, ch // TILE, trace_tile, 0)

    rad = dot_nt(basis[...], ft[...])
    rad = rad[0:nb] + rad[2 * nb:3 * nb]
    for l in range(3):
        radgz[g, l] = rad[:, l * ch:(l + 1) * ch].astype(BF16)
    rgz = []
    for d in range(1, ngz):
        rgz.append(pltpu.make_async_remote_copy(
            src_ref=radgz.at[g], dst_ref=radgz.at[g],
            send_sem=rgz_s.at[d], recv_sem=rgz_r.at[d],
            device_id=at(d, 0), device_id_type=MESH))
    for c in rgz:
        c.start()

    for c in mrs:
        c.wait_recv()
    mixgz[g] = added(mixrs).astype(mixgz.dtype)
    mgz = []
    for d in range(1, ngz):
        mgz.append(pltpu.make_async_remote_copy(
            src_ref=mixgz.at[g], dst_ref=mixgz.at[g],
            send_sem=mgz_s.at[d], recv_sem=mgz_r.at[d],
            device_id=at(d, 0), device_id_type=MESH))
    for c in mgz:
        c.start()

    back = []

    def scatter(first, last):
        res = dot_nt(oh[first * hb:last * hb, :], con[...])
        for pos in range(first, last):
            block = res[(pos - first) * hb:(pos - first + 1) * hb]
            gsend[pos, 0:hb] = block[:, :ch].astype(BF16)
            gsend[pos, hb:2 * hb] = block[:, ch:].astype(BF16)
            s = ORDER[pos]
            copy = pltpu.make_async_remote_copy(
                src_ref=gsend.at[pos], dst_ref=grecv.at[pos],
                send_sem=back_s.at[pos], recv_sem=back_r.at[pos],
                device_id=at(s // 3 - 1, s % 3 - 1), device_id_type=MESH)
            copy.start()
            back.append(copy)

    scatter(0, 3)

    for c in rgz:
        c.wait_recv()
    radxy[b] = added(radgz).astype(BF16)
    rxy = []
    for d in range(1, nxy):
        rxy.append(pltpu.make_async_remote_copy(
            src_ref=radxy.at[b], dst_ref=radxy.at[b],
            send_sem=rxy_s.at[d], recv_sem=rxy_r.at[d],
            device_id=at(0, d), device_id_type=MESH))
    for c in rxy:
        c.start()

    scatter(3, 6)

    for c in mgz:
        c.wait_recv()
    mixag[b] = added(mixgz).astype(mixag.dtype)
    mag = []
    for d in range(1, nxy):
        mag.append(pltpu.make_async_remote_copy(
            src_ref=mixag.at[b], dst_ref=mixag.at[b],
            send_sem=mag_s.at[d], recv_sem=mag_r.at[d],
            device_id=at(0, d), device_id_type=MESH))
    for c in mag:
        c.start()

    scatter(6, 8)
    kept = dot_nt(oh[8 * hb:9 * hb, :], con[...])
    agrad_ref[0, 0, 0:hb] = kept[:, :ch]
    agrad_ref[0, 0, hb:2 * hb] = kept[:, ch:]

    for c in rxy:
        c.wait_recv()
    rgrad_ref[...] = added(radxy)

    for c in back:
        c.wait_recv()
    for h in range(2):
        part = agrad_ref[0, 0, h * hb:(h + 1) * hb]
        for pos in range(8):
            part = part + grecv[pos, h * hb:(h + 1) * hb].astype(F32)
        agrad_ref[0, 0, h * hb:(h + 1) * hb] = part
    for c in mag:
        c.wait_recv()
    for i in range(nxy):
        mgrad_ref[:, i * rows:(i + 1) * rows, :] = mixag[i].astype(F32)
    for c in halo + mrs + rgz + mgz + back + rxy + mag:
        c.wait_send()


def shards(cotangent, displacement, neighbours, counts, atom_feat, radial_weight, mix_weight):
    ngz, nxy = lax.axis_size("gz"), lax.axis_size("xy")
    nk, npr = neighbours.shape[2:]
    natom, ch = atom_feat.shape[2:]
    nb = radial_weight.shape[1]
    hb = natom // 2
    slots = nk * npr
    rows = ch // nxy
    sent = F32 if rows % 16 else BF16
    V = pltpu.VMEM
    dma = pltpu.SemaphoreType.DMA
    vm = pl.BlockSpec(memory_space=pltpu.VMEM)
    return pl.pallas_call(
        functools.partial(kernel, ngz, nxy),
        out_shape=(
            jax.ShapeDtypeStruct((1, 1, natom, ch), F32),
            jax.ShapeDtypeStruct((3, nb, ch), F32),
            jax.ShapeDtypeStruct((3, ch, ch), F32),
        ),
        in_specs=[pl.BlockSpec(memory_space=pltpu.HBM)] * 7,
        out_specs=(vm, vm, vm),
        scratch_shapes=[
            V((2 * ch, 9 * hb), BF16),
            V((9 * hb, slots), BF16),
            V((9, nk, npr), F32),
            V((nk, npr), jnp.int32),
            V((9, nk, npr), F32),
            V((nk, npr), F32),
            V((nk, npr), F32),
            V((3 * nb, slots), BF16),
            V((128, 3 * ch), F32),
            V((3 * ch, 128), BF16),
            V((nk, 3 * ch, npr), F32),
            V((nk, ch, npr), F32),
            V((9, ch, npr), F32),
            V((3, ch, ch), BF16),
            V((ch, 9 * npr), BF16),
            V((9, ch, npr), F32),
            V((3 * ch, slots), BF16),
            V((2 * ch, slots), BF16),
            V((8, natom, ch), BF16),
            V((8, natom, ch), BF16),
            V((nxy, 3, rows, ch), sent),
            V((nxy, 3, rows, ch), sent),
            V((ngz, 3, rows, ch), sent),
            V((nxy, 3, rows, ch), sent),
            V((ngz, 3, nb, ch), BF16),
            V((nxy, 3, nb, ch), BF16),
            dma((8,)), dma((8,)), dma((8,)), dma((8,)),
            dma((nxy,)), dma((nxy,)), dma((ngz,)), dma((ngz,)), dma((nxy,)), dma((nxy,)),
            dma((ngz,)), dma((ngz,)), dma((nxy,)), dma((nxy,)),
            V(atom_feat.shape, BF16), V(neighbours.shape, jnp.int32), V(displacement.shape, F32),
            V(counts.shape, jnp.int32), V(radial_weight.shape, F32), V(mix_weight.shape, BF16),
            V(cotangent.shape, BF16), dma((7,)),
        ],
        compiler_params=pltpu.CompilerParams(
            collective_id=0, has_side_effects=True, vmem_limit_bytes=48 * 1024 * 1024
        ),
    )(cotangent, displacement, neighbours, counts, atom_feat, radial_weight, mix_weight)


def solution(mesh):
    in_specs = (
        P("gz", "xy", None, None, None),
        P("gz", "xy", None, None, None),
        P("gz", "xy", None, None),
        P("gz", "xy", None),
        P("gz", "xy", None, None),
        P(),
        P(),
    )
    out_specs = (P("gz", "xy", None, None), P(), P())
    return jax.shard_map(shards, mesh=mesh, in_specs=in_specs, out_specs=out_specs, check_vma=False)
```

```python
import functools
import math

import jax
import jax.numpy as jnp
from jax import lax
from jax.experimental import pallas as pl
from jax.experimental.pallas import tpu as pltpu
from jax.sharding import PartitionSpec as P

CUTOFF = 4.0
LEVEL_SPANS = ((0, 1), (1, 4), (4, 9))
LEVEL_OF = (0, 1, 1, 1, 2, 2, 2, 2, 2)
ORDER = (0, 1, 2, 6, 7, 8, 3, 5, 4)
MESH = pl.DeviceIdType.MESH
TILE = 32
UNROLL = 8
PREP = 4
GATHER = 16
EARLY = 3
NT = (((1,), (1,)), ((), ()))
F32 = jnp.float32
BF16 = jnp.bfloat16


def dot(a, b):
    return jnp.dot(a, b, preferred_element_type=F32)


def dot_nt(a, b):
    return lax.dot_general(a, b, NT, preferred_element_type=F32)


def added(ref):
    total = ref[0].astype(F32)
    for i in range(1, ref.shape[0]):
        total = total + ref[i].astype(F32)
    return total


def kernel(
    ngz, nxy,
    cot_hbm, disp_hbm, nbr_hbm, cnt_hbm, atom_hbm, rw_hbm, mw_hbm,
    agrad_ref, rgrad_ref, mgrad_ref,
    tbl, oh, key, half, ang, dist, env, basis, wpad, wt, radial, feat, cott, mixt,
    mom, dmom, ft, con, gsend, grecv, mixp, mixrs, mixgz, mixag, radgz, radxy,
    halo_s, halo_r, back_s, back_r, mrs_s, mrs_r, mgz_s, mgz_r, mag_s, mag_r,
    rgz_s, rgz_r, rxy_s, rxy_r,
    atom_ref, nbr_ref, disp_ref, cnt_ref, rw_ref, mw_ref, cot_ref, load_s,
):
    g = lax.axis_index("gz")
    b = lax.axis_index("xy")
    nk, npr = nbr_ref.shape[2], nbr_ref.shape[3]
    ch = atom_ref.shape[3]
    hb = atom_ref.shape[2] // 2
    nb = rw_ref.shape[1]
    rows = ch // nxy

    def at(dg, db):
        return (lax.rem(g + dg + ngz, ngz), lax.rem(b + db + nxy, nxy))

    loads = [
        pltpu.make_async_copy(src, dst, load_s.at[i])
        for i, (src, dst) in enumerate((
            (atom_hbm, atom_ref), (nbr_hbm, nbr_ref), (disp_hbm, disp_ref), (cnt_hbm, cnt_ref),
            (rw_hbm, rw_ref), (mw_hbm, mw_ref), (cot_hbm, cot_ref),
        ))
    ]
    for c in loads:
        c.start()

    barrier = pltpu.get_barrier_semaphore()
    peers = [(0, d) for d in range(1, nxy)] + [(d, 0) for d in range(1, ngz)]
    peers += [(-1, -1), (-1, 1), (1, -1), (1, 1)]
    for dg, db in peers:
        pl.semaphore_signal(barrier, inc=1, device_id=at(dg, db), device_id_type=MESH)

    own = pl.ds(8 * hb, hb)
    loads[0].wait()
    for h in range(2):
        tbl[h * ch:(h + 1) * ch, own] = (
            atom_ref[0, 0, h * hb:(h + 1) * hb, :].astype(F32).T.astype(BF16)
        )
    for c in loads[1:]:
        c.wait()
    n = nbr_ref[0, 0]
    low = lax.bitwise_and(n, hb - 1)
    slot = lax.shift_right_logical(n, int(math.log2(2 * hb)))
    for pos in range(9):
        key[pos] = jnp.where(slot == ORDER[pos], low, -1).astype(F32)
    half[...] = lax.bitwise_and(n, hb)
    x = disp_ref[0, 0, 0] * (1.0 / CUTOFF)
    y = disp_ref[0, 0, 1] * (1.0 / CUTOFF)
    z = disp_ref[0, 0, 2] * (1.0 / CUTOFF)
    mask = (lax.broadcasted_iota(jnp.int32, (nk, npr), 0) < cnt_ref[0]).astype(F32)
    r3, r5, r15 = math.sqrt(3.0), math.sqrt(5.0), math.sqrt(15.0)
    comps = (
        None, r3 * x, r3 * y, r3 * z, r15 * x * y, r15 * y * z,
        0.5 * r5 * (2.0 * z * z - x * x - y * y), r15 * x * z, 0.5 * r15 * (x * x - y * y),
    )
    for m in range(9):
        ang[m] = mask if m == 0 else comps[m] * mask
    d0, d1, d2 = disp_ref[0, 0, 0], disp_ref[0, 0, 1], disp_ref[0, 0, 2]
    r = jnp.sqrt(d0 * d0 + d1 * d1 + d2 * d2)
    dist[...] = r
    env[...] = 0.5 * (jnp.cos(r * (math.pi / CUTOFF)) + 1.0)

    wpad[...] = jnp.zeros(wpad.shape, F32)
    for l in range(3):
        w = rw_ref[l]
        hi = w.astype(BF16).astype(F32)
        lanes = slice(l * ch, (l + 1) * ch)
        wpad[0:nb, lanes] = hi
        wpad[nb:2 * nb, lanes] = w - hi
        wpad[2 * nb:3 * nb, lanes] = hi
        wt[lanes, :] = wpad[:, lanes].T.astype(BF16)
        mixt[l] = mw_ref[l].astype(F32).T.astype(BF16)
    for m in range(9):
        cott[m] = cot_ref[0, 0, m].astype(F32).T

    step = CUTOFF / (nb - 1)
    sharp = ((nb - 1) / CUTOFF) ** 2
    centres = lax.broadcasted_iota(jnp.int32, (nb, npr), 0).astype(F32) * step
    lines = lax.broadcasted_iota(jnp.int32, (hb, npr), 0).astype(F32).astype(BF16)
    one = jnp.ones((hb, npr), BF16)
    zero = jnp.zeros((hb, npr), BF16)

    def lanes_of(k, count=1):
        return pl.ds(pl.multiple_of(k * npr, npr), count * npr)

    def prepare(c, carry):
        for j in range(PREP):
            k = c * PREP + j
            at_k = lanes_of(k)
            off = dist[pl.ds(k, 1), :] - centres
            shaped = jnp.exp(-sharp * (off * off)) * env[pl.ds(k, 1), :]
            hi = shaped.astype(BF16)
            basis[0:nb, at_k] = hi
            basis[nb:2 * nb, at_k] = hi
            basis[2 * nb:3 * nb, at_k] = (shaped - hi.astype(F32)).astype(BF16)
            for pos in range(9):
                row = jnp.broadcast_to(key[pos, pl.ds(k, 1), :], (hb, npr)).astype(BF16)
                oh[pos * hb:(pos + 1) * hb, at_k] = jnp.where(lines == row, one, zero)
        rad = dot(wt[:, 0:3 * nb], basis[:, lanes_of(c * PREP, PREP)])
        for j in range(PREP):
            radial[c * PREP + j] = rad[:, j * npr:(j + 1) * npr]
        return carry

    lax.fori_loop(0, EARLY, prepare, 0)

    pl.semaphore_wait(barrier, len(peers))

    halo = []
    for pos in range(8):
        s = ORDER[pos]
        dg, db = s // 3 - 1, s % 3 - 1
        halo.append(pltpu.make_async_remote_copy(
            src_ref=tbl.at[:, own], dst_ref=tbl.at[:, pl.ds(pos * hb, hb)],
            send_sem=halo_s.at[pos], recv_sem=halo_r.at[pos],
            device_id=at(-dg, -db), device_id_type=MESH))
    for c in halo[5:] + halo[:5]:
        c.start()

    lax.fori_loop(EARLY, nk // PREP, prepare, 0)

    def gather(first, last, more):
        def step(c, carry):
            both = dot(tbl[:, first * hb:last * hb],
                       oh[first * hb:last * hb, lanes_of(c * GATHER, GATHER)])
            for j in range(GATHER):
                k = c * GATHER + j
                cols = slice(j * npr, (j + 1) * npr)
                upper = half[pl.ds(k, 1), :] > 0
                got = jnp.where(upper, both[ch:, cols], both[:ch, cols])
                feat[k] = feat[k] + got if more else got
            return carry

        lax.fori_loop(0, nk // GATHER, step, 0)

    for c in halo[5:]:
        c.wait_recv()
    gather(5, 9, False)
    for c in halo[:5]:
        c.wait_recv()
    gather(0, 5, True)

    def moment_tile(t, carry):
        at_t = pl.ds(pl.multiple_of(t * TILE, TILE), TILE)

        def body(k, acc):
            f = feat[k, at_t, :]
            w = [
                radial[k, pl.ds(pl.multiple_of(l * ch + t * TILE, TILE), TILE), :] * f
                for l in range(3)
            ]
            return tuple(
                acc[m] + ang[m, pl.ds(k, 1), :] * w[LEVEL_OF[m]] for m in range(9)
            )

        acc = lax.fori_loop(0, nk, body, tuple(jnp.zeros((TILE, npr), F32) for _ in range(9)),
                            unroll=UNROLL)
        for m in range(9):
            mom[at_t, m * npr:(m + 1) * npr] = acc[m].astype(BF16)
        return carry

    lax.fori_loop(0, ch // TILE, moment_tile, 0)

    scalar = dot(mixt[0], mom[:, 0:npr])
    gating = jax.nn.sigmoid(scalar)
    slope = gating * (1.0 - gating)
    inner = jnp.zeros((ch, npr), F32)
    dmx = [None] * 9
    for m in range(1, 9):
        inner = inner + cott[m] * dot(mixt[LEVEL_OF[m]], mom[:, m * npr:(m + 1) * npr])
        dmx[m] = (cott[m] * gating).astype(BF16)
    dmx[0] = (cott[0] * (gating + scalar * slope) + inner * slope).astype(BF16)
    for l, (lo, hi) in enumerate(LEVEL_SPANS):
        total = None
        for m in range(lo, hi):
            part = dot_nt(mom[:, m * npr:(m + 1) * npr], dmx[m])
            total = part if total is None else total + part
        for i in range(nxy):
            mixp[i, l] = total[i * rows:(i + 1) * rows].astype(mixp.dtype)

    mixrs[b] = mixp[b]
    mrs = []
    for d in range(1, nxy):
        to = lax.rem(b + d, nxy)
        mrs.append(pltpu.make_async_remote_copy(
            src_ref=mixp.at[to],
            dst_ref=mixrs.at[b],
            send_sem=mrs_s.at[d], recv_sem=mrs_r.at[d],
            device_id=(g, to), device_id_type=MESH))
    for c in mrs:
        c.start()

    for m in range(9):
        dmom[m] = dot(mw_ref[LEVEL_OF[m]], dmx[m]).astype(BF16).astype(F32)

    def trace_tile(t, carry):
        at_t = pl.ds(pl.multiple_of(t * TILE, TILE), TILE)
        dm = [dmom[m, at_t, :] for m in range(9)]

        def body(k, carry):
            f = feat[k, at_t, :]
            at_k = lanes_of(k)
            total = None
            for l, (lo, hi) in enumerate(LEVEL_SPANS):
                tr = None
                for m in range(lo, hi):
                    part = ang[m, pl.ds(k, 1), :] * dm[m]
                    tr = part if tr is None else tr + part
                at_l = pl.ds(pl.multiple_of(l * ch + t * TILE, TILE), TILE)
                part = radial[k, at_l, :] * tr
                total = part if total is None else total + part
                ft[at_l, at_k] = (f * tr).astype(BF16)
            upper = half[pl.ds(k, 1), :] > 0
            con[at_t, at_k] = jnp.where(upper, 0.0, total).astype(BF16)
            con[pl.ds(pl.multiple_of(ch + t * TILE, TILE), TILE), at_k] = (
                jnp.where(upper, total, 0.0).astype(BF16)
            )
            return carry

        return lax.fori_loop(0, nk, body, carry, unroll=UNROLL)

    lax.fori_loop(0, ch // TILE, trace_tile, 0)

    back = []

    def scatter(first, last):
        res = dot_nt(oh[first * hb:last * hb, :], con[...])
        for pos in range(first, last):
            block = res[(pos - first) * hb:(pos - first + 1) * hb]
            gsend[pos, 0:hb] = block[:, :ch].astype(BF16)
            gsend[pos, hb:2 * hb] = block[:, ch:].astype(BF16)
            s = ORDER[pos]
            copy = pltpu.make_async_remote_copy(
                src_ref=gsend.at[pos], dst_ref=grecv.at[pos],
                send_sem=back_s.at[pos], recv_sem=back_r.at[pos],
                device_id=at(s // 3 - 1, s % 3 - 1), device_id_type=MESH)
            copy.start()
            back.append(copy)

    scatter(0, 3)

    rad = dot_nt(basis[...], ft[...])
    rad = rad[0:nb] + rad[2 * nb:3 * nb]
    for l in range(3):
        radgz[g, l] = rad[:, l * ch:(l + 1) * ch].astype(BF16)
    rgz = []
    for d in range(1, ngz):
        rgz.append(pltpu.make_async_remote_copy(
            src_ref=radgz.at[g], dst_ref=radgz.at[g],
            send_sem=rgz_s.at[d], recv_sem=rgz_r.at[d],
            device_id=at(d, 0), device_id_type=MESH))
    for c in rgz:
        c.start()

    for c in mrs:
        c.wait_recv()
    mixgz[g] = added(mixrs).astype(mixgz.dtype)
    mgz = []
    for d in range(1, ngz):
        mgz.append(pltpu.make_async_remote_copy(
            src_ref=mixgz.at[g], dst_ref=mixgz.at[g],
            send_sem=mgz_s.at[d], recv_sem=mgz_r.at[d],
            device_id=at(d, 0), device_id_type=MESH))
    for c in mgz:
        c.start()

    scatter(3, 6)

    for c in rgz:
        c.wait_recv()
    radxy[b] = added(radgz).astype(BF16)
    rxy = []
    for d in range(1, nxy):
        rxy.append(pltpu.make_async_remote_copy(
            src_ref=radxy.at[b], dst_ref=radxy.at[b],
            send_sem=rxy_s.at[d], recv_sem=rxy_r.at[d],
            device_id=at(0, d), device_id_type=MESH))
    for c in rxy:
        c.start()

    for c in mgz:
        c.wait_recv()
    mixag[b] = added(mixgz).astype(mixag.dtype)
    mag = []
    for d in range(1, nxy):
        mag.append(pltpu.make_async_remote_copy(
            src_ref=mixag.at[b], dst_ref=mixag.at[b],
            send_sem=mag_s.at[d], recv_sem=mag_r.at[d],
            device_id=at(0, d), device_id_type=MESH))
    for c in mag:
        c.start()

    scatter(6, 8)
    kept = dot_nt(oh[8 * hb:9 * hb, :], con[...])
    agrad_ref[0, 0, 0:hb] = kept[:, :ch]
    agrad_ref[0, 0, hb:2 * hb] = kept[:, ch:]

    for c in rxy:
        c.wait_recv()
    rgrad_ref[...] = added(radxy)

    for c in back:
        c.wait_recv()
    for h in range(2):
        part = agrad_ref[0, 0, h * hb:(h + 1) * hb]
        for pos in range(8):
            part = part + grecv[pos, h * hb:(h + 1) * hb].astype(F32)
        agrad_ref[0, 0, h * hb:(h + 1) * hb] = part
    for c in mag:
        c.wait_recv()
    for i in range(nxy):
        mgrad_ref[:, i * rows:(i + 1) * rows, :] = mixag[i].astype(F32)
    for c in halo + mrs + rgz + mgz + back + rxy + mag:
        c.wait_send()


def shards(cotangent, displacement, neighbours, counts, atom_feat, radial_weight, mix_weight):
    ngz, nxy = lax.axis_size("gz"), lax.axis_size("xy")
    nk, npr = neighbours.shape[2:]
    natom, ch = atom_feat.shape[2:]
    nb = radial_weight.shape[1]
    hb = natom // 2
    slots = nk * npr
    rows = ch // nxy
    sent = F32 if rows % 16 else BF16
    V = pltpu.VMEM
    dma = pltpu.SemaphoreType.DMA
    vm = pl.BlockSpec(memory_space=pltpu.VMEM)
    return pl.pallas_call(
        functools.partial(kernel, ngz, nxy),
        out_shape=(
            jax.ShapeDtypeStruct((1, 1, natom, ch), F32),
            jax.ShapeDtypeStruct((3, nb, ch), F32),
            jax.ShapeDtypeStruct((3, ch, ch), F32),
        ),
        in_specs=[pl.BlockSpec(memory_space=pltpu.HBM)] * 7,
        out_specs=(vm, vm, vm),
        scratch_shapes=[
            V((2 * ch, 9 * hb), BF16),
            V((9 * hb, slots), BF16),
            V((9, nk, npr), F32),
            V((nk, npr), jnp.int32),
            V((9, nk, npr), F32),
            V((nk, npr), F32),
            V((nk, npr), F32),
            V((3 * nb, slots), BF16),
            V((128, 3 * ch), F32),
            V((3 * ch, 128), BF16),
            V((nk, 3 * ch, npr), F32),
            V((nk, ch, npr), F32),
            V((9, ch, npr), F32),
            V((3, ch, ch), BF16),
            V((ch, 9 * npr), BF16),
            V((9, ch, npr), F32),
            V((3 * ch, slots), BF16),
            V((2 * ch, slots), BF16),
            V((8, natom, ch), BF16),
            V((8, natom, ch), BF16),
            V((nxy, 3, rows, ch), sent),
            V((nxy, 3, rows, ch), sent),
            V((ngz, 3, rows, ch), sent),
            V((nxy, 3, rows, ch), sent),
            V((ngz, 3, nb, ch), BF16),
            V((nxy, 3, nb, ch), BF16),
            dma((8,)), dma((8,)), dma((8,)), dma((8,)),
            dma((nxy,)), dma((nxy,)), dma((ngz,)), dma((ngz,)), dma((nxy,)), dma((nxy,)),
            dma((ngz,)), dma((ngz,)), dma((nxy,)), dma((nxy,)),
            V(atom_feat.shape, BF16), V(neighbours.shape, jnp.int32), V(displacement.shape, F32),
            V(counts.shape, jnp.int32), V(radial_weight.shape, F32), V(mix_weight.shape, BF16),
            V(cotangent.shape, BF16), dma((7,)),
        ],
        compiler_params=pltpu.CompilerParams(
            collective_id=0, has_side_effects=True, vmem_limit_bytes=48 * 1024 * 1024
        ),
    )(cotangent, displacement, neighbours, counts, atom_feat, radial_weight, mix_weight)


def solution(mesh):
    in_specs = (
        P("gz", "xy", None, None, None),
        P("gz", "xy", None, None, None),
        P("gz", "xy", None, None),
        P("gz", "xy", None),
        P("gz", "xy", None, None),
        P(),
        P(),
    )
    out_specs = (P("gz", "xy", None, None), P(), P())
    return jax.shard_map(shards, mesh=mesh, in_specs=in_specs, out_specs=out_specs, check_vma=False)
```
